32 devices in a mesh: parts: 2 (over x), gy: 16 (over z, y, core).
Axes of the slice: x: 2, y: 2, z: 4, core: 2. Of those that a mesh axis runs over, the one named last changes fastest.
Arguments:
- measured: bfloat16 [8, 32, 256, 128], P(None, None, ('parts', 'gy')), parts along dimension 2, may hold values from 0.19921875 to 8
- start: float32 [32, 256, 128], P(None, ('parts', 'gy')), parts along dimension 1, may hold values from 0.5 to 4
- psf: float32 [8, 15, 7, 7], replicated, may hold values from 0.05 to 1
- background: float32 [8], replicated, may hold values from 0.2 to 2
Outputs:
- estimate: float32 [32, 256, 128], P(None, ('parts', 'gy')), parts along dimension 1
The draws below stay inside these ranges and needn't reach their ends.
There are 2 independent parts, one for each index of `parts`. The reference program is written for one: setup_inputs(seed, part) draws one part's arguments, and reference() takes and returns one part's arrays. A program takes and returns all parts, laid end to end along the dimension named above; an argument that names none is the same for every part. Nothing has to cross between parts.
All inputs are finite; a program needn't handle non-finite values.
Results may differ from the reference program's by a relative error of at most 0.0003.
Values may be sent and summed in bfloat16 or wider, within the bound.
A program may use at most 128 MiB of HBM per device.

```python
import math
import jax
import jax.numpy as jnp
from jax import lax

VIEWS = 8
KZ = 15
KY = 7
KX = 7
PLANES = 32
COLS = 128
ITERS = 1
ROWS = 128


def block_levels(stream_key, dims, cuts, low, high):
    loudness = 1.0
    for dim, shards_of in cuts:
        heights = jax.random.uniform(jax.random.fold_in(jax.random.fold_in(stream_key, 6), dim), (shards_of,), jnp.float32, low / len(cuts), high / len(cuts))
        loudness = loudness * jnp.repeat(jnp.exp(heights), dims[dim] // shards_of).reshape((-1,) + (1,) * (len(dims) - 1 - dim))
    return loudness


def setup_inputs(seed: int = 0, part: int = 0) -> dict:
    splits = jax.random.split(jax.random.key(seed), 5)
    part_keys = jax.random.split(jax.random.fold_in(splits[4], part), 5)
    return {
        "measured": jnp.clip(jnp.exp(math.log(8.0) - 3.6927934 * jax.random.uniform(part_keys[0], (VIEWS, PLANES, ROWS, COLS), jnp.float32) ** block_levels(part_keys[0], (VIEWS, PLANES, ROWS, COLS), ((2, 16),), -0.2, 0.2)), 0.19921875, 8.0).astype(jnp.bfloat16),
        "start": jnp.clip(jnp.exp(math.log(4.0) - 2.0794415 * jax.random.uniform(part_keys[1], (PLANES, ROWS, COLS), jnp.float32) ** block_levels(part_keys[1], (PLANES, ROWS, COLS), ((1, 16),), -0.2, 0.2)), 0.5, 4.0),
        "psf": jnp.clip(jnp.exp(jax.random.uniform(splits[2], (VIEWS, KZ, KY, KX), jnp.float32, math.log(0.05), math.log(1.0))), 0.05, 1.0),
        "background": jnp.clip(jnp.exp(jax.random.uniform(splits[3], (VIEWS,), jnp.float32, math.log(0.2), math.log(2.0))), 0.2, 2.0),
    }


def build_weights(psf, planes):
    kernel = psf / jnp.sum(psf, axis=(1, 2, 3), keepdims=True)
    rounded_kernel = lax.optimization_barrier(kernel.astype(jnp.bfloat16)).astype(jnp.float32)
    depth = psf.shape[1]
    plane_index = jnp.arange(planes, dtype=jnp.int32)
    tap_index = jnp.arange(depth, dtype=jnp.int32)
    onehot = (plane_index[None, :, None] - plane_index[None, None, :] + depth // 2 == tap_index[:, None, None]).astype(jnp.float32)
    views, reach_y, reach_x = psf.shape[0], psf.shape[2], psf.shape[3]
    blur_w = jnp.einsum("vabc,apq->bvpcq", rounded_kernel, onehot, precision=lax.Precision.HIGHEST)
    blur_w = blur_w.reshape(reach_y, views * planes, reach_x * planes).astype(jnp.bfloat16)
    corr_w = jnp.einsum("vabc,apq->vbqcp", rounded_kernel, onehot, precision=lax.Precision.HIGHEST)
    corr_w = corr_w.reshape(views, reach_y, planes, reach_x * planes).astype(jnp.bfloat16)
    return blur_w, corr_w


def column_table(cols, reach_x, sign):
    half_x = reach_x // 2
    source = jnp.arange(cols, dtype=jnp.int32)[:, None, None]
    tap = jnp.arange(reach_x, dtype=jnp.int32)[None, :, None]
    target = jnp.arange(cols, dtype=jnp.int32)[None, None, :]
    table = (source == target + sign * (tap - half_x)).astype(jnp.bfloat16)
    return table.reshape(cols, reach_x * cols)


def blur_rows(padded, blur_w):
    planes, rows_in, cols = padded.shape
    reach_y = blur_w.shape[0]
    reach_x = blur_w.shape[2] // planes
    rows_out = rows_in - 2 * (reach_y // 2)
    table = column_table(cols, reach_x, -1)
    shifted = jnp.dot(padded.reshape(planes * rows_in, cols), table, preferred_element_type=jnp.float32)
    shifted = shifted.astype(jnp.bfloat16).reshape(planes, rows_in, reach_x, cols)
    weights = blur_w.reshape(reach_y, blur_w.shape[1], reach_x, planes)
    result = jnp.zeros((blur_w.shape[1], rows_out, cols), jnp.float32)
    for shift_y in range(reach_y):
        lines = shifted[:, reach_y - 1 - shift_y:reach_y - 1 - shift_y + rows_out]
        result = result + jnp.einsum("ocp,prcx->orx", weights[shift_y], lines, preferred_element_type=jnp.float32)
    return result.reshape(-1, planes, rows_out, cols)


def correlate_rows(padded, corr_w):
    views, planes, rows_in, cols = padded.shape
    reach_y = corr_w.shape[1]
    reach_x = corr_w.shape[3] // planes
    rows_out = rows_in - 2 * (reach_y // 2)
    table = column_table(cols, reach_x, 1)
    shifted = jnp.dot(padded.reshape(views * planes * rows_in, cols), table, preferred_element_type=jnp.float32)
    shifted = shifted.astype(jnp.bfloat16).reshape(views, planes, rows_in, reach_x, cols)
    weights = corr_w.reshape(views, reach_y, planes, reach_x, planes)
    total = jnp.zeros((planes, rows_out, cols), jnp.float32)
    for shift_y in range(reach_y):
        lines = shifted[:, :, shift_y:shift_y + rows_out]
        total = total + jnp.einsum("vqcp,vprcx->qrx", weights[:, shift_y], lines, preferred_element_type=jnp.float32)
    return total


def reference(measured, start, psf, background):
    blur_w, corr_w = build_weights(psf, PLANES)
    half_y = KY // 2
    recorded = measured.astype(jnp.float32)
    estimate = start
    for step in range(ITERS):
        rounded = estimate.astype(jnp.bfloat16)
        padded = jnp.pad(rounded, ((0, 0), (half_y, half_y), (0, 0)))
        blurred = blur_rows(padded, blur_w)
        ratio = (recorded / (blurred + background[:, None, None, None])).astype(jnp.bfloat16)
        ratio_pad = jnp.pad(ratio, ((0, 0), (0, 0), (half_y, half_y), (0, 0)))
        total = correlate_rows(ratio_pad, corr_w)
        estimate = estimate * total / VIEWS
    return estimate
```

```python
import functools

import jax
import jax.numpy as jnp
from jax import lax
from jax.experimental import pallas as pl
from jax.experimental.pallas import tpu as pltpu
from jax.sharding import PartitionSpec as P

F32 = jnp.float32
BF16 = jnp.bfloat16


def shift_cols(x, by):
    cols = x.shape[1]
    if by == 0:
        return x
    lane = lax.broadcasted_iota(jnp.int32, x.shape, 1)
    rolled = pltpu.roll(x, (-by) % cols, 1)
    keep = lane < cols - by if by > 0 else lane >= -by
    return jnp.where(keep, rolled, 0.0)


def kernel(
    dims, measured, start, psf, background, out,
    taps, corr_w, blur_w, rows_pad, shifted, recorded, ratio, sent, got,
    send_sem, recv_sem,
):
    views, depth, ky, kx, planes, rows, cols, size = dims
    hz, hy, hx = depth // 2, ky // 2, kx // 2
    wide = views * planes
    me = lax.axis_index("gy")
    has_prev = me > 0
    has_next = me < size - 1
    prev = {"gy": jnp.maximum(me - 1, 0)}
    nxt = {"gy": jnp.minimum(me + 1, size - 1)}

    barrier = pltpu.get_barrier_semaphore()

    @pl.when(has_prev)
    def _():
        pl.semaphore_signal(barrier, inc=1, device_id=prev, device_id_type=pl.DeviceIdType.MESH)

    @pl.when(has_next)
    def _():
        pl.semaphore_signal(barrier, inc=1, device_id=nxt, device_id_type=pl.DeviceIdType.MESH)

    for y in range(rows):
        rows_pad[hy + y] = start[:, y, :].astype(BF16)

    def halo(to_prev):
        if to_prev:
            src, dst = rows_pad.at[pl.ds(hy, hy)], rows_pad.at[pl.ds(hy + rows, hy)]
        else:
            src, dst = rows_pad.at[pl.ds(rows, hy)], rows_pad.at[pl.ds(0, hy)]
        i = 0 if to_prev else 1
        return pltpu.make_async_remote_copy(
            src_ref=src, dst_ref=dst, send_sem=send_sem.at[i], recv_sem=recv_sem.at[i],
            device_id=prev if to_prev else nxt, device_id_type=pl.DeviceIdType.MESH,
        )

    def partial(to_prev):
        i = 0 if to_prev else 1
        return pltpu.make_async_remote_copy(
            src_ref=sent.at[i], dst_ref=got.at[i], send_sem=send_sem.at[2 + i], recv_sem=recv_sem.at[2 + i],
            device_id=prev if to_prev else nxt, device_id_type=pl.DeviceIdType.MESH,
        )

    pl.semaphore_wait(barrier, (me + size - 1) // size + (2 * size - 2 - me) // size)

    @pl.when(has_prev)
    def _():
        halo(True).start()

    @pl.when(has_next)
    def _():
        halo(False).start()

    total = jnp.sum(jnp.sum(psf[...], axis=(0, 1)), axis=1, keepdims=True)
    taps[:, :, :depth] = (psf[...] / total).astype(BF16).astype(F32).reshape(ky * kx, views, depth)
    per_tile = 128 // planes
    lane = lax.broadcasted_iota(jnp.int32, (ky * kx, 128), 1)
    tiles = []
    for first in range(0, views, per_tile):
        tile = jnp.zeros((ky * kx, 128), F32)
        for j in range(per_tile):
            part = taps[:, first + j, :]
            if j:
                part = pltpu.roll(part, j * planes, 1)
            tile = jnp.where((lane >= j * planes) & (lane < j * planes + depth), part, tile)
        tiles.append(tile)
    flat = jnp.concatenate(tiles, axis=1)
    corr_w[kx * planes :] = jnp.zeros((wide - kx * planes, ky * wide), BF16)
    q_of = lax.broadcasted_iota(jnp.int32, (planes, wide), 0)
    p_of = lax.broadcasted_iota(jnp.int32, (planes, wide), 1) % planes
    band = jnp.abs(p_of - q_of) <= hz
    eye = (
        lax.broadcasted_iota(jnp.int32, (wide, wide), 0)
        == lax.broadcasted_iota(jnp.int32, (wide, wide), 1)
    ).astype(BF16)
    for b in range(ky):
        for c in range(kx):
            i = b * kx + c
            line = jnp.broadcast_to(flat[i : i + 1], (planes, wide))
            line = pltpu.roll(line, wide - hz, 1, stride=1, stride_axis=0)
            corr_w[c * planes : (c + 1) * planes, b * wide : (b + 1) * wide] = jnp.where(band, line, 0.0).astype(BF16)
        blur_w[:, b * wide : (b + 1) * wide] = lax.dot_general(
            eye, corr_w[:, b * wide : (b + 1) * wide], (((1,), (1,)), ((), ())), preferred_element_type=F32
        ).astype(BF16)

    recorded[...] = measured[...].astype(F32)
    ratio[:, :cols] = jnp.zeros((wide, cols), BF16)
    ratio[:, (rows + 1) * cols :] = jnp.zeros((wide, cols), BF16)
    shifted[kx * planes :] = jnp.zeros((wide - kx * planes, (rows + 2 * hy) * cols), BF16)

    def spread(y):
        line = rows_pad[y].astype(F32)
        for c in range(kx):
            shifted[c * planes : (c + 1) * planes, y * cols : (y + 1) * cols] = shift_cols(line, hx - c).astype(BF16)

    for y in range(hy, hy + rows):
        spread(y)

    @pl.when(has_prev)
    def _():
        halo(True).wait_send()
        halo(False).wait_recv()

    @pl.when(jnp.logical_not(has_prev))
    def _():
        rows_pad[:hy] = jnp.zeros((hy, planes, cols), BF16)

    @pl.when(has_next)
    def _():
        halo(False).wait_send()
        halo(True).wait_recv()

    @pl.when(jnp.logical_not(has_next))
    def _():
        rows_pad[hy + rows :] = jnp.zeros((hy, planes, cols), BF16)

    for y in range(hy):
        spread(y)
        spread(hy + rows + y)

    offsets = jnp.concatenate([jnp.full((planes, cols), background[v], F32) for v in range(views)], axis=0)
    for t in range(rows // 2):
        operand = jnp.concatenate(
            [shifted[:, (2 * t + ky - 1 - b) * cols : (2 * t + ky + 1 - b) * cols] for b in range(ky)], axis=0
        )
        blurred = jnp.dot(blur_w[...], operand, preferred_element_type=F32)
        for j in range(2):
            y = 2 * t + j
            below = blurred[:, j * cols : (j + 1) * cols] + offsets
            ratio[:, (y + 1) * cols : (y + 2) * cols] = (recorded[:, y, :] / below).astype(BF16)

    def correlate(r):
        used = [b for b in range(ky) if -1 <= r + b - hy <= rows - 1]
        weights = jnp.concatenate([corr_w[: kx * planes, b * wide : (b + 1) * wide] for b in used], axis=1)
        operand = jnp.concatenate(
            [ratio[:, (r + b - hy + 1) * cols : (r + b - hy + 3) * cols] for b in used], axis=0
        )
        every = jnp.dot(weights, operand, preferred_element_type=F32)
        results = []
        for j in range(2):
            total = jnp.zeros((planes, cols), F32)
            for c in range(kx):
                total += shift_cols(every[c * planes : (c + 1) * planes, j * cols : (j + 1) * cols], c - hx)
            results.append(total)
        return results

    _, sent[0, 0] = correlate(-4)
    sent[0, 1], sent[0, 2] = correlate(-2)

    @pl.when(has_prev)
    def _():
        partial(True).start()

    sent[1, 0], sent[1, 1] = correlate(rows)
    sent[1, 2], _ = correlate(rows + 2)

    @pl.when(has_next)
    def _():
        partial(False).start()

    for t in range(rows // 2):
        out[:, 2 * t, :], out[:, 2 * t + 1, :] = correlate(2 * t)

    @pl.when(has_prev)
    def _():
        partial(False).wait_recv()
        for y in range(hy):
            out[:, y, :] += got[1, y]
        partial(True).wait_send()

    @pl.when(has_next)
    def _():
        partial(True).wait_recv()
        for y in range(hy):
            out[:, rows - hy + y, :] += got[0, y]
        partial(False).wait_send()


def local(size, measured, start, psf, background):
    views, planes, rows, cols = measured.shape
    _, depth, ky, kx = psf.shape
    hy = ky // 2
    wide = views * planes
    dims = (views, depth, ky, kx, planes, rows, cols, size)
    total = pl.pallas_call(
        functools.partial(kernel, dims),
        out_shape=jax.ShapeDtypeStruct((planes, rows, cols), F32),
        in_specs=[pl.BlockSpec(memory_space=pltpu.VMEM)] * 3 + [pl.BlockSpec(memory_space=pltpu.SMEM)],
        out_specs=pl.BlockSpec(memory_space=pltpu.VMEM),
        scratch_shapes=[
            pltpu.VMEM((ky * kx, views, 128), F32),
            pltpu.VMEM((wide, ky * wide), BF16),
            pltpu.VMEM((wide, ky * wide), BF16),
            pltpu.VMEM((rows + 2 * hy, planes, cols), BF16),
            pltpu.VMEM((wide, (rows + 2 * hy) * cols), BF16),
            pltpu.VMEM((wide, rows, cols), F32),
            pltpu.VMEM((wide, (rows + 2) * cols), BF16),
            pltpu.VMEM((2, hy, planes, cols), F32),
            pltpu.VMEM((2, hy, planes, cols), F32),
            pltpu.SemaphoreType.DMA((4,)),
            pltpu.SemaphoreType.DMA((4,)),
        ],
        compiler_params=pltpu.CompilerParams(
            collective_id=0, has_side_effects=True, vmem_limit_bytes=48 * 1024 * 1024
        ),
    )(measured.reshape(wide, rows, cols), start, jnp.transpose(psf, (2, 3, 0, 1)), background)
    return start * total / views


def solution(mesh):
    in_specs = (P(None, None, ("parts", "gy"), None), P(None, ("parts", "gy"), None), P(), P())
    out_specs = P(None, ("parts", "gy"), None)
    body = functools.partial(local, mesh.shape["gy"])
    return jax.shard_map(body, mesh=mesh, in_specs=in_specs, out_specs=out_specs, check_vma=False)
```

```python
import functools

import jax
import jax.numpy as jnp
from jax import lax
from jax.experimental import pallas as pl
from jax.experimental.pallas import tpu as pltpu
from jax.sharding import PartitionSpec as P

F32 = jnp.float32
BF16 = jnp.bfloat16


def shift_cols(x, by):
    cols = x.shape[1]
    if by == 0:
        return x
    lane = lax.broadcasted_iota(jnp.int32, x.shape, 1)
    rolled = pltpu.roll(x, (-by) % cols, 1)
    keep = lane < cols - by if by > 0 else lane >= -by
    return jnp.where(keep, rolled, 0.0)


def kernel(
    dims, measured_hbm, start_hbm, psf_hbm, background_hbm, out,
    measured, start, psf, background, taps, corr_w, blur_w, rows_pad, shifted, recorded, ratio, sent, got,
    send_sem, recv_sem, load_sem,
):
    views, depth, ky, kx, planes, rows, cols, size = dims
    hz, hy, hx = depth // 2, ky // 2, kx // 2
    wide = views * planes
    me = lax.axis_index("gy")
    has_prev = me > 0
    has_next = me < size - 1
    prev = {"gy": jnp.maximum(me - 1, 0)}
    nxt = {"gy": jnp.minimum(me + 1, size - 1)}

    loads = [
        pltpu.make_async_copy(src, dst, load_sem.at[i])
        for i, (src, dst) in enumerate(
            [(start_hbm, start), (psf_hbm, psf), (measured_hbm, measured), (background_hbm, background)]
        )
    ]
    loads[0].start()
    loads[1].start()

    barrier = pltpu.get_barrier_semaphore()

    @pl.when(has_prev)
    def _():
        pl.semaphore_signal(barrier, inc=1, device_id=prev, device_id_type=pl.DeviceIdType.MESH)

    @pl.when(has_next)
    def _():
        pl.semaphore_signal(barrier, inc=1, device_id=nxt, device_id_type=pl.DeviceIdType.MESH)

    loads[0].wait()
    loads[2].start()
    loads[3].start()
    for y in range(rows):
        rows_pad[hy + y] = start[:, y, :].astype(BF16)

    def halo(to_prev):
        if to_prev:
            src, dst = rows_pad.at[pl.ds(hy, hy)], rows_pad.at[pl.ds(hy + rows, hy)]
        else:
            src, dst = rows_pad.at[pl.ds(rows, hy)], rows_pad.at[pl.ds(0, hy)]
        i = 0 if to_prev else 1
        return pltpu.make_async_remote_copy(
            src_ref=src, dst_ref=dst, send_sem=send_sem.at[i], recv_sem=recv_sem.at[i],
            device_id=prev if to_prev else nxt, device_id_type=pl.DeviceIdType.MESH,
        )

    def partial(to_prev):
        i = 0 if to_prev else 1
        return pltpu.make_async_remote_copy(
            src_ref=sent.at[i], dst_ref=got.at[i], send_sem=send_sem.at[2 + i], recv_sem=recv_sem.at[2 + i],
            device_id=prev if to_prev else nxt, device_id_type=pl.DeviceIdType.MESH,
        )

    pl.semaphore_wait(barrier, (me + size - 1) // size + (2 * size - 2 - me) // size)

    @pl.when(has_prev)
    def _():
        halo(True).start()

    @pl.when(has_next)
    def _():
        halo(False).start()

    loads[1].wait()
    total = jnp.sum(jnp.sum(psf[...], axis=(0, 1)), axis=1, keepdims=True)
    taps[:, :, :depth] = (psf[...] / total).astype(BF16).astype(F32).reshape(ky * kx, views, depth)
    per_tile = 128 // planes
    lane = lax.broadcasted_iota(jnp.int32, (ky * kx, 128), 1)
    tiles = []
    for first in range(0, views, per_tile):
        tile = jnp.zeros((ky * kx, 128), F32)
        for j in range(per_tile):
            part = taps[:, first + j, :]
            if j:
                part = pltpu.roll(part, j * planes, 1)
            tile = jnp.where((lane >= j * planes) & (lane < j * planes + depth), part, tile)
        tiles.append(tile)
    flat = jnp.concatenate(tiles, axis=1)
    corr_w[kx * planes :] = jnp.zeros((wide - kx * planes, ky * wide), BF16)
    q_of = lax.broadcasted_iota(jnp.int32, (planes, wide), 0)
    p_of = lax.broadcasted_iota(jnp.int32, (planes, wide), 1) % planes
    band = jnp.abs(p_of - q_of) <= hz
    eye = (
        lax.broadcasted_iota(jnp.int32, (wide, wide), 0)
        == lax.broadcasted_iota(jnp.int32, (wide, wide), 1)
    ).astype(BF16)
    for b in range(ky):
        for c in range(kx):
            i = b * kx + c
            line = jnp.broadcast_to(flat[i : i + 1], (planes, wide))
            line = pltpu.roll(line, wide - hz, 1, stride=1, stride_axis=0)
            corr_w[c * planes : (c + 1) * planes, b * wide : (b + 1) * wide] = jnp.where(band, line, 0.0).astype(BF16)
        blur_w[:, b * wide : (b + 1) * wide] = lax.dot_general(
            eye, corr_w[:, b * wide : (b + 1) * wide], (((1,), (1,)), ((), ())), preferred_element_type=F32
        ).astype(BF16)

    loads[2].wait()
    loads[3].wait()
    recorded[...] = measured[...].astype(F32)
    ratio[:, :cols] = jnp.zeros((wide, cols), BF16)
    ratio[:, (rows + 1) * cols :] = jnp.zeros((wide, cols), BF16)
    shifted[kx * planes :] = jnp.zeros((wide - kx * planes, (rows + 2 * hy) * cols), BF16)

    def spread(y):
        line = rows_pad[y].astype(F32)
        for c in range(kx):
            shifted[c * planes : (c + 1) * planes, y * cols : (y + 1) * cols] = shift_cols(line, hx - c).astype(BF16)

    for y in range(hy, hy + rows):
        spread(y)

    offsets = jnp.concatenate([jnp.full((planes, cols), background[v], F32) for v in range(views)], axis=0)

    def blur(t):
        operand = jnp.concatenate(
            [shifted[:, (2 * t + ky - 1 - b) * cols : (2 * t + ky + 1 - b) * cols] for b in range(ky)], axis=0
        )
        blurred = jnp.dot(blur_w[...], operand, preferred_element_type=F32)
        for j in range(2):
            y = 2 * t + j
            below = blurred[:, j * cols : (j + 1) * cols] + offsets
            ratio[:, (y + 1) * cols : (y + 2) * cols] = (recorded[:, y, :] / below).astype(BF16)

    def correlate(r):
        used = [b for b in range(ky) if -1 <= r + b - hy <= rows - 1]
        weights = jnp.concatenate([corr_w[: kx * planes, b * wide : (b + 1) * wide] for b in used], axis=1)
        operand = jnp.concatenate(
            [ratio[:, (r + b - hy + 1) * cols : (r + b - hy + 3) * cols] for b in used], axis=0
        )
        every = jnp.dot(weights, operand, preferred_element_type=F32)
        results = []
        for j in range(2):
            total = jnp.zeros((planes, cols), F32)
            for c in range(kx):
                total += shift_cols(every[c * planes : (c + 1) * planes, j * cols : (j + 1) * cols], c - hx)
            results.append(total)
        return results

    @pl.when(has_prev)
    def _():
        halo(False).wait_recv()

    @pl.when(jnp.logical_not(has_prev))
    def _():
        rows_pad[:hy] = jnp.zeros((hy, planes, cols), BF16)

    for y in range(hy):
        spread(y)
    for t in range((hy + 1) // 2):
        blur(t)
    _, sent[0, 0] = correlate(-4)
    sent[0, 1], sent[0, 2] = correlate(-2)

    @pl.when(has_prev)
    def _():
        partial(True).start()

    @pl.when(has_next)
    def _():
        halo(True).wait_recv()

    @pl.when(jnp.logical_not(has_next))
    def _():
        rows_pad[hy + rows :] = jnp.zeros((hy, planes, cols), BF16)

    for y in range(hy):
        spread(hy + rows + y)
    for t in range(rows // 2 - 1, (hy + 1) // 2 - 1, -1):
        blur(t)
    sent[1, 0], sent[1, 1] = correlate(rows)
    sent[1, 2], _ = correlate(rows + 2)

    @pl.when(has_next)
    def _():
        partial(False).start()

    for t in range(rows // 2):
        out[:, 2 * t, :], out[:, 2 * t + 1, :] = correlate(2 * t)

    @pl.when(has_prev)
    def _():
        partial(False).wait_recv()
        for y in range(hy):
            out[:, y, :] += got[1, y]
        partial(True).wait_send()
        halo(True).wait_send()

    @pl.when(has_next)
    def _():
        partial(True).wait_recv()
        for y in range(hy):
            out[:, rows - hy + y, :] += got[0, y]
        partial(False).wait_send()
        halo(False).wait_send()


def local(size, measured, start, psf, background):
    views, planes, rows, cols = measured.shape
    _, depth, ky, kx = psf.shape
    hy = ky // 2
    wide = views * planes
    dims = (views, depth, ky, kx, planes, rows, cols, size)
    total = pl.pallas_call(
        functools.partial(kernel, dims),
        out_shape=jax.ShapeDtypeStruct((planes, rows, cols), F32),
        in_specs=[pl.BlockSpec(memory_space=pltpu.HBM)] * 4,
        out_specs=pl.BlockSpec(memory_space=pltpu.VMEM),
        scratch_shapes=[
            pltpu.VMEM((wide, rows, cols), BF16),
            pltpu.VMEM((planes, rows, cols), F32),
            pltpu.VMEM((ky, kx, views, depth), F32),
            pltpu.SMEM((views,), F32),
            pltpu.VMEM((ky * kx, views, 128), F32),
            pltpu.VMEM((wide, ky * wide), BF16),
            pltpu.VMEM((wide, ky * wide), BF16),
            pltpu.VMEM((rows + 2 * hy, planes, cols), BF16),
            pltpu.VMEM((wide, (rows + 2 * hy) * cols), BF16),
            pltpu.VMEM((wide, rows, cols), F32),
            pltpu.VMEM((wide, (rows + 2) * cols), BF16),
            pltpu.VMEM((2, hy, planes, cols), F32),
            pltpu.VMEM((2, hy, planes, cols), F32),
            pltpu.SemaphoreType.DMA((4,)),
            pltpu.SemaphoreType.DMA((4,)),
            pltpu.SemaphoreType.DMA((4,)),
        ],
        compiler_params=pltpu.CompilerParams(
            collective_id=0, has_side_effects=True, vmem_limit_bytes=63 * 1024 * 1024
        ),
    )(measured.reshape(wide, rows, cols), start, jnp.transpose(psf, (2, 3, 0, 1)), background)
    return start * total / views


def solution(mesh):
    in_specs = (P(None, None, ("parts", "gy"), None), P(None, ("parts", "gy"), None), P(), P())
    out_specs = P(None, ("parts", "gy"), None)
    body = functools.partial(local, mesh.shape["gy"])
    return jax.shard_map(body, mesh=mesh, in_specs=in_specs, out_specs=out_specs, check_vma=False)
```

```python
import functools

import jax
import jax.numpy as jnp
from jax import lax
from jax.experimental import pallas as pl
from jax.experimental.pallas import tpu as pltpu
from jax.sharding import PartitionSpec as P

F32 = jnp.float32
BF16 = jnp.bfloat16


def shift_cols(x, by):
    cols = x.shape[1]
    if by == 0:
        return x
    lane = lax.broadcasted_iota(jnp.int32, x.shape, 1)
    rolled = pltpu.roll(x, (-by) % cols, 1)
    keep = lane < cols - by if by > 0 else lane >= -by
    return jnp.where(keep, rolled, 0.0)


def kernel(
    dims, measured_hbm, start_hbm, psf_hbm, background_hbm, out,
    measured, start, psf, background, taps, corr_w, blur_w, rows_pad, shifted, recorded, ratio, sent, got,
    send_sem, recv_sem, load_sem,
):
    views, depth, ky, kx, planes, rows, cols, size = dims
    hz, hy, hx = depth // 2, ky // 2, kx // 2
    wide = views * planes
    me = lax.axis_index("gy")
    has_prev = me > 0
    has_next = me < size - 1
    prev = {"gy": jnp.maximum(me - 1, 0)}
    nxt = {"gy": jnp.minimum(me + 1, size - 1)}

    loads = [
        pltpu.make_async_copy(src, dst, load_sem.at[i])
        for i, (src, dst) in enumerate(
            [(start_hbm, start), (psf_hbm, psf), (measured_hbm, measured), (background_hbm, background)]
        )
    ]
    loads[0].start()
    loads[1].start()

    barrier = pltpu.get_barrier_semaphore()

    @pl.when(has_prev)
    def _():
        pl.semaphore_signal(barrier, inc=1, device_id=prev, device_id_type=pl.DeviceIdType.MESH)

    @pl.when(has_next)
    def _():
        pl.semaphore_signal(barrier, inc=1, device_id=nxt, device_id_type=pl.DeviceIdType.MESH)

    loads[0].wait()
    loads[2].start()
    loads[3].start()
    for y in range(rows):
        rows_pad[hy + y] = start[:, y, :].astype(BF16)

    def halo(to_prev):
        if to_prev:
            src, dst = rows_pad.at[pl.ds(hy, hy)], rows_pad.at[pl.ds(hy + rows, hy)]
        else:
            src, dst = rows_pad.at[pl.ds(rows, hy)], rows_pad.at[pl.ds(0, hy)]
        i = 0 if to_prev else 1
        return pltpu.make_async_remote_copy(
            src_ref=src, dst_ref=dst, send_sem=send_sem.at[i], recv_sem=recv_sem.at[i],
            device_id=prev if to_prev else nxt, device_id_type=pl.DeviceIdType.MESH,
        )

    def partial(to_prev):
        i = 0 if to_prev else 1
        return pltpu.make_async_remote_copy(
            src_ref=sent.at[i], dst_ref=got.at[i], send_sem=send_sem.at[2 + i], recv_sem=recv_sem.at[2 + i],
            device_id=prev if to_prev else nxt, device_id_type=pl.DeviceIdType.MESH,
        )

    pl.semaphore_wait(barrier, (me + size - 1) // size + (2 * size - 2 - me) // size)

    @pl.when(has_prev)
    def _():
        halo(True).start()

    @pl.when(has_next)
    def _():
        halo(False).start()

    loads[1].wait()
    total = jnp.sum(jnp.sum(psf[...], axis=(0, 1)), axis=1, keepdims=True)
    taps[:, :, :depth] = (psf[...] / total).astype(BF16).astype(F32).reshape(ky * kx, views, depth)
    per_tile = 128 // planes
    lane = lax.broadcasted_iota(jnp.int32, (ky * kx, 128), 1)
    tiles = []
    for first in range(0, views, per_tile):
        tile = jnp.zeros((ky * kx, 128), F32)
        for j in range(per_tile):
            part = taps[:, first + j, :]
            if j:
                part = pltpu.roll(part, j * planes, 1)
            tile = jnp.where((lane >= j * planes) & (lane < j * planes + depth), part, tile)
        tiles.append(tile)
    flat = jnp.concatenate(tiles, axis=1)
    corr_w[kx * planes :] = jnp.zeros((wide - kx * planes, ky * wide), BF16)
    q_of = lax.broadcasted_iota(jnp.int32, (planes, wide), 0)
    p_of = lax.broadcasted_iota(jnp.int32, (planes, wide), 1) % planes
    band = jnp.abs(p_of - q_of) <= hz
    for b in range(ky):
        for c in range(kx):
            i = b * kx + c
            line = jnp.broadcast_to(flat[i : i + 1], (planes, wide))
            line = pltpu.roll(line, wide - hz, 1, stride=1, stride_axis=0)
            corr_w[c * planes : (c + 1) * planes, b * wide : (b + 1) * wide] = jnp.where(band, line, 0.0).astype(BF16)
        blur_w[:, b * wide : (b + 1) * wide] = corr_w[:, b * wide : (b + 1) * wide].T

    loads[2].wait()
    loads[3].wait()
    recorded[...] = measured[...].astype(F32)
    ratio[:, :cols] = jnp.zeros((wide, cols), BF16)
    ratio[:, (rows + 1) * cols :] = jnp.zeros((wide, cols), BF16)
    shifted[kx * planes :] = jnp.zeros((wide - kx * planes, (rows + 2 * hy) * cols), BF16)

    def spread(y):
        line = rows_pad[y].astype(F32)
        for c in range(kx):
            shifted[c * planes : (c + 1) * planes, y * cols : (y + 1) * cols] = shift_cols(line, hx - c).astype(BF16)

    for y in range(hy, hy + rows):
        spread(y)

    offsets = jnp.concatenate([jnp.full((planes, cols), background[v], F32) for v in range(views)], axis=0)

    def blur(t):
        operand = jnp.concatenate(
            [shifted[:, (2 * t + ky - 1 - b) * cols : (2 * t + ky + 1 - b) * cols] for b in range(ky)], axis=0
        )
        blurred = jnp.dot(blur_w[...], operand, preferred_element_type=F32)
        for j in range(2):
            y = 2 * t + j
            below = blurred[:, j * cols : (j + 1) * cols] + offsets
            ratio[:, (y + 1) * cols : (y + 2) * cols] = (recorded[:, y, :] / below).astype(BF16)

    def correlate(r):
        used = [b for b in range(ky) if -1 <= r + b - hy <= rows - 1]
        weights = jnp.concatenate([corr_w[: kx * planes, b * wide : (b + 1) * wide] for b in used], axis=1)
        operand = jnp.concatenate(
            [ratio[:, (r + b - hy + 1) * cols : (r + b - hy + 3) * cols] for b in used], axis=0
        )
        every = jnp.dot(weights, operand, preferred_element_type=F32)
        results = []
        for j in range(2):
            total = jnp.zeros((planes, cols), F32)
            for c in range(kx):
                total += shift_cols(every[c * planes : (c + 1) * planes, j * cols : (j + 1) * cols], c - hx)
            results.append(total)
        return results

    @pl.when(has_prev)
    def _():
        halo(False).wait_recv()

    @pl.when(jnp.logical_not(has_prev))
    def _():
        rows_pad[:hy] = jnp.zeros((hy, planes, cols), BF16)

    for y in range(hy):
        spread(y)
    for t in range((hy + 1) // 2):
        blur(t)
    _, sent[0, 0] = correlate(-4)
    sent[0, 1], sent[0, 2] = correlate(-2)

    @pl.when(has_prev)
    def _():
        partial(True).start()

    @pl.when(has_next)
    def _():
        halo(True).wait_recv()

    @pl.when(jnp.logical_not(has_next))
    def _():
        rows_pad[hy + rows :] = jnp.zeros((hy, planes, cols), BF16)

    for y in range(hy):
        spread(hy + rows + y)
    for t in range(rows // 2 - 1, (hy + 1) // 2 - 1, -1):
        blur(t)
    sent[1, 0], sent[1, 1] = correlate(rows)
    sent[1, 2], _ = correlate(rows + 2)

    @pl.when(has_next)
    def _():
        partial(False).start()

    for t in range(rows // 2):
        out[:, 2 * t, :], out[:, 2 * t + 1, :] = correlate(2 * t)

    @pl.when(has_prev)
    def _():
        partial(False).wait_recv()
        for y in range(hy):
            out[:, y, :] += got[1, y]
        partial(True).wait_send()
        halo(True).wait_send()

    @pl.when(has_next)
    def _():
        partial(True).wait_recv()
        for y in range(hy):
            out[:, rows - hy + y, :] += got[0, y]
        partial(False).wait_send()
        halo(False).wait_send()


def local(size, measured, start, psf, background):
    views, planes, rows, cols = measured.shape
    _, depth, ky, kx = psf.shape
    hy = ky // 2
    wide = views * planes
    dims = (views, depth, ky, kx, planes, rows, cols, size)
    total = pl.pallas_call(
        functools.partial(kernel, dims),
        out_shape=pltpu.VMEM((planes, rows, cols), F32),
        in_specs=[pl.BlockSpec(memory_space=pltpu.HBM)] * 4,
        out_specs=pl.BlockSpec(memory_space=pltpu.VMEM),
        scratch_shapes=[
            pltpu.VMEM((wide, rows, cols), BF16),
            pltpu.VMEM((planes, rows, cols), F32),
            pltpu.VMEM((ky, kx, views, depth), F32),
            pltpu.SMEM((views,), F32),
            pltpu.VMEM((ky * kx, views, 128), F32),
            pltpu.VMEM((wide, ky * wide), BF16),
            pltpu.VMEM((wide, ky * wide), BF16),
            pltpu.VMEM((rows + 2 * hy, planes, cols), BF16),
            pltpu.VMEM((wide, (rows + 2 * hy) * cols), BF16),
            pltpu.VMEM((wide, rows, cols), F32),
            pltpu.VMEM((wide, (rows + 2) * cols), BF16),
            pltpu.VMEM((2, hy, planes, cols), F32),
            pltpu.VMEM((2, hy, planes, cols), F32),
            pltpu.SemaphoreType.DMA((4,)),
            pltpu.SemaphoreType.DMA((4,)),
            pltpu.SemaphoreType.DMA((4,)),
        ],
        compiler_params=pltpu.CompilerParams(
            collective_id=0, has_side_effects=True, vmem_limit_bytes=63 * 1024 * 1024
        ),
    )(measured.reshape(wide, rows, cols), start, jnp.transpose(psf, (2, 3, 0, 1)), background)
    return start * total / views


def solution(mesh):
    in_specs = (P(None, None, ("parts", "gy"), None), P(None, ("parts", "gy"), None), P(), P())
    out_specs = P(None, ("parts", "gy"), None)
    body = functools.partial(local, mesh.shape["gy"])
    return jax.shard_map(body, mesh=mesh, in_specs=in_specs, out_specs=out_specs, check_vma=False)
```
